32 devices in a mesh: ens: 2 (over y), lat: 16 (over z, x, core).
Axes of the slice: x: 2, y: 2, z: 4, core: 2. Of those that a mesh axis runs over, the one named last changes fastest.
Arguments:
- field: bfloat16 [128, 1440, 384], P(('ens', 'lat')), parts along dimension 0, may hold values from -6 to 6
- norm_gain: float32 [384], replicated, may hold values from 0.1 to 1.9
- legendre_fwd: bfloat16 [256, 256, 64], P('lat'), as said below
- legendre_inv: bfloat16 [256, 256, 64], P('lat')
- degree_gain: float32 [256, 384], replicated, may hold values from 0.5 to 2
- mix_weight: bfloat16 [2, 384, 384], replicated, may hold values from -0.21875 to 0.21875
- mlp_gain: float32 [384], replicated, may hold values from 0.1 to 1.9
- up_weight: bfloat16 [384, 768], replicated, may hold values from -0.3125 to 0.3125
- up_bias: float32 [768], replicated, may hold values from -4 to 4
- down_weight: bfloat16 [768, 384], replicated, may hold values from -0.21875 to 0.21875
Outputs:
- result: bfloat16 [128, 1440, 384], P(('ens', 'lat')), parts along dimension 0
The draws below stay inside these ranges and needn't reach their ends.
There are 2 independent parts, one for each index of `ens`. The reference program is written for one: setup_inputs(seed, part) draws one part's arguments, and reference() takes and returns one part's arrays. A program takes and returns all parts, laid end to end along the dimension named above; an argument that names none is the same for every part. Nothing has to cross between parts.
Inputs may be any that keep to these rules, and one draw needn't show every extreme that they name: legendre_inv holds orthonormal associated Legendre functions of degree l and order m (zero where l < m) at the grid's colatitudes, legendre_fwd the same times each row's quadrature weight.
All inputs are finite; a program needn't handle non-finite values.
Results may differ from the reference program's by a relative error of at most 0.009.
Values may be sent and summed in bfloat16 or wider, within the bound.
No kernel may reach another device: no remote copies, remote signals or barrier semaphores. Data moves between devices by JAX's collectives and lax.ppermute only.
A program may use at most 64 MiB of HBM per device.

```python
import math
import jax
import jax.numpy as jnp
from jax import lax

C = 384
NLON = 1440
MLP_WIDTH = 768
MMAX = 256
LAT_DEV = 4
LMAX = 256
LATITUDE_ROWS = 64
N_LAT = 16


def legendre_tables(key):
    jitter = 0.4
    shift = jax.random.uniform(jax.random.fold_in(key, 7), (LATITUDE_ROWS,), jnp.float32)
    rows = jnp.arange(LATITUDE_ROWS, dtype=jnp.int32).astype(jnp.float32)
    colatitude_angle = math.pi * (rows + 0.5 + jitter * (shift - 0.5)) / LATITUDE_ROWS
    zval = jnp.cos(colatitude_angle)[None, :]
    sine_value = jnp.sin(colatitude_angle)[None, :]
    quadrature_weight = math.pi / LATITUDE_ROWS * sine_value
    harmonic_order = jnp.arange(MMAX, dtype=jnp.int32).astype(jnp.float32)[:, None]
    ks = jnp.arange(1, MMAX, dtype=jnp.int32).astype(jnp.float32)
    partial_logs = jnp.concatenate([jnp.zeros((1,), jnp.float32), jnp.cumsum(jnp.log((2.0 * ks - 1.0) / (2.0 * ks)))])[:, None]
    log_norm_factor = 0.5 * jnp.log((2.0 * harmonic_order + 1.0) / (4.0 * math.pi)) + 0.5 * partial_logs
    diagonal_terms = jnp.exp(log_norm_factor + harmonic_order * jnp.log(sine_value))

    def step(carry, degree):
        before, last = carry
        lval = degree.astype(jnp.float32)
        alpha = jnp.sqrt((4.0 * lval * lval - 1.0) / jnp.maximum(lval * lval - harmonic_order * harmonic_order, 1.0))
        beta = jnp.sqrt(jnp.maximum((lval - 1.0) ** 2 - harmonic_order * harmonic_order, 0.0) / jnp.maximum(4.0 * (lval - 1.0) ** 2 - 1.0, 1.0))
        recur = alpha * (zval * last - beta * before)
        value = jnp.where(lval < harmonic_order, 0.0, jnp.where(lval == harmonic_order, diagonal_terms, recur))
        return ((last, value), value)
    start = jnp.zeros((MMAX, LATITUDE_ROWS), jnp.float32)
    unused, values = lax.scan(step, (start, start), jnp.arange(LMAX, dtype=jnp.int32))
    table = jnp.transpose(values, (1, 0, 2))
    return (table, table * quadrature_weight[None, :, :])


def draw_legendre_fwd(key, part):
    return legendre_tables(key)[1].astype(jnp.bfloat16)


def draw_legendre_inv(key, part):
    return legendre_tables(key)[0].astype(jnp.bfloat16)


def shard_levels(stream_key, extent, shards, low, top_value):
    factor_of = 1.0
    for axis_at, parts in shards:
        heights = jax.random.uniform(jax.random.fold_in(jax.random.fold_in(stream_key, 6), axis_at), (parts,), jnp.float32, low / len(shards), top_value / len(shards))
        factor_of = factor_of * jnp.repeat(jnp.exp(heights), extent[axis_at] // parts).reshape((-1,) + (1,) * (len(extent) - 1 - axis_at))
    return factor_of


def gaussian(rng, extent, width, most, cuts=(), kind=jnp.bfloat16):
    values = width * jax.random.normal(rng, extent, jnp.float32)
    if cuts:
        values = values * shard_levels(rng, extent, cuts, -0.22, 0.18)
    return jnp.clip(values, -most, most).astype(kind)


def setup_inputs(seed: int = 0, part: int = 0) -> dict:
    splits = jax.random.split(jax.random.key(seed), 11)
    own_keys = jax.random.split(jax.random.fold_in(splits[10], part), 11)
    field = gaussian(own_keys[0], (LATITUDE_ROWS, NLON, C), 1.0, 6.0, ((0, 16),))
    norm_gain = jnp.clip(1.0 + 0.18 * jax.random.normal(splits[1], (C,), jnp.float32), 0.1, 1.9)
    legendre_fwd = draw_legendre_fwd(jax.random.fold_in(splits[10], 71), part)
    legendre_inv = draw_legendre_inv(jax.random.fold_in(splits[10], 71), part)
    degree_gain = jnp.clip(jnp.exp(jax.random.uniform(splits[4], (LMAX, C), jnp.float32, math.log(0.5), math.log(2.0))), 0.5, 2.0)
    mix_weight = gaussian(splits[5], (2, C, C), (2 * C) ** -0.5, 0.21875)
    mlp_gain = jnp.clip(1.0 + 0.18 * jax.random.normal(splits[6], (C,), jnp.float32), 0.1, 1.9)
    up_weight = gaussian(splits[7], (C, MLP_WIDTH), C ** -0.5, 0.3125)
    up_bias = gaussian(splits[8], (MLP_WIDTH,), 0.7, 4.0, (), jnp.float32)
    down_weight = gaussian(splits[9], (MLP_WIDTH, C), MLP_WIDTH ** -0.5, 0.21875)
    return dict(field=field, norm_gain=norm_gain, legendre_fwd=legendre_fwd, legendre_inv=legendre_inv, degree_gain=degree_gain, mix_weight=mix_weight, mlp_gain=mlp_gain, up_weight=up_weight, up_bias=up_bias, down_weight=down_weight)


def dft_tables(nlon, modes):
    lon = jnp.arange(nlon, dtype=jnp.int32)
    wave = jnp.arange(modes, dtype=jnp.int32)
    phase = (wave[:, None] * lon[None, :] % nlon).astype(jnp.float32) * (2.0 * math.pi / nlon)
    scale = 2.0 * math.pi / nlon
    forward = jnp.stack([scale * jnp.cos(phase), -scale * jnp.sin(phase)], axis=1).reshape(2 * modes, nlon)
    weight = jnp.where(wave == 0, 1.0, 2.0).astype(jnp.float32)[:, None]
    inverse = jnp.stack([weight * jnp.cos(phase), -weight * jnp.sin(phase)], axis=1).reshape(2 * modes, nlon)
    return (forward.astype(jnp.bfloat16), inverse.T.astype(jnp.bfloat16))

def layer_norm(values, gain):
    values = values.astype(jnp.float32)
    center = values - lax.optimization_barrier(jnp.mean(values, axis=-1, keepdims=True))
    spread = lax.optimization_barrier(jnp.mean(center * center, axis=-1, keepdims=True))
    return center * lax.rsqrt(spread + 1e-05) * gain

def reference(field, norm_gain, legendre_fwd, legendre_inv, degree_gain, mix_weight, mlp_gain, up_weight, up_bias, down_weight):
    forward, inverse = dft_tables(NLON, MMAX)
    blocks = field.reshape(N_LAT, LAT_DEV, NLON, C)

    def analyse(block):
        normed = layer_norm(block, norm_gain).astype(jnp.bfloat16)
        spec = jnp.einsum('nk,jkc->jnc', forward.astype(jnp.float32), normed.astype(jnp.float32))
        return spec.astype(jnp.bfloat16)
    spectrum_lon = lax.map(analyse, blocks).reshape(LATITUDE_ROWS, MMAX, 2, C)
    coeffs = jnp.einsum('mlj,jmrc->mlrc', legendre_fwd.astype(jnp.float32), spectrum_lon.astype(jnp.float32))
    scaled = (coeffs * degree_gain[None, :, None, :]).astype(jnp.bfloat16).reshape(MMAX * LMAX, 2 * C)
    block_w = jnp.concatenate([jnp.concatenate([mix_weight[0], mix_weight[1]], 1), jnp.concatenate([-mix_weight[1], mix_weight[0]], 1)], 0)
    mixed = jnp.dot(scaled, block_w, preferred_element_type=jnp.float32).astype(jnp.bfloat16).reshape(MMAX, LMAX, 2, C)
    synth_lon = jnp.einsum('mlj,mlrc->jmrc', legendre_inv.astype(jnp.float32), mixed.astype(jnp.float32)).astype(jnp.bfloat16)
    synth_blocks = synth_lon.reshape(N_LAT, LAT_DEV, 2 * MMAX, C)

    def finish(pair):
        block, synth = pair
        normed = layer_norm(block, norm_gain).astype(jnp.bfloat16)
        filtered = jnp.einsum('kn,jnc->jkc', inverse.astype(jnp.float32), synth.astype(jnp.float32))
        inner = filtered + normed.astype(jnp.float32)
        post = layer_norm(inner, mlp_gain).astype(jnp.bfloat16).reshape(LAT_DEV * NLON, C)
        hidden = jax.nn.gelu(jnp.dot(post, up_weight, preferred_element_type=jnp.float32) + up_bias).astype(jnp.bfloat16)
        out = block.reshape(LAT_DEV * NLON, C).astype(jnp.float32) + jnp.dot(hidden, down_weight, preferred_element_type=jnp.float32)
        return out.astype(jnp.bfloat16).reshape(LAT_DEV, NLON, C)
    return lax.map(finish, (blocks, synth_blocks)).reshape(LATITUDE_ROWS, NLON, C)
```

```python
import functools
import math

import jax
import jax.numpy as jnp
import ml_dtypes
import numpy as np
from jax import lax
from jax.experimental import pallas as pl
from jax.experimental.pallas import tpu as pltpu
from jax.sharding import PartitionSpec as P

BF = jnp.bfloat16
F32 = jnp.float32
EPS = 1e-05
VMEM_LIMIT = 48 * 1024 * 1024


def tables(nlon, modes):
    lon = np.arange(nlon)
    wave = np.arange(modes)
    phase = (wave[:, None] * lon[None, :] % nlon) * (2.0 * math.pi / nlon)
    scale = 2.0 * math.pi / nlon
    weight = np.where(wave == 0, 1.0, 2.0)[:, None]
    forward = np.concatenate([scale * np.cos(phase), -scale * np.sin(phase)], 0)
    inverse = np.concatenate([weight * np.cos(phase), -weight * np.sin(phase)], 0).T
    as_bf = lambda a: a.astype(np.float32).astype(ml_dtypes.bfloat16)
    return as_bf(forward), as_bf(inverse)


def dot(a, b):
    return jnp.dot(a, b, preferred_element_type=F32)


def norm(values, gain):
    center = values - jnp.mean(values, axis=-1, keepdims=True)
    spread = jnp.mean(center * center, axis=-1, keepdims=True)
    return center * lax.rsqrt(spread + EPS) * gain


def analyse_kernel(field_ref, gain_ref, table_ref, spec_ref, normed_ref):
    modes = table_ref.shape[0] // 2
    chan = field_ref.shape[-1]
    normed = norm(field_ref[0].astype(F32), gain_ref[...]).astype(BF)
    normed_ref[0] = normed
    spec = dot(table_ref[...], normed).astype(BF)
    shape = spec_ref.shape[:1] + spec_ref.shape[2:3] + (chan,)
    spec_ref[:, 0, :, :chan] = spec[:modes].reshape(shape)
    spec_ref[:, 0, :, chan:] = spec[modes:].reshape(shape)


def analyse(field, gain, table, devices, modes_here):
    rows, nlon, chan = field.shape
    modes2 = table.shape[0]
    return pl.pallas_call(
        analyse_kernel,
        grid=(rows,),
        in_specs=[
            pl.BlockSpec((1, nlon, chan), lambda j: (j, 0, 0)),
            pl.BlockSpec((1, chan), lambda j: (0, 0)),
            pl.BlockSpec((modes2, nlon), lambda j: (0, 0)),
        ],
        out_specs=[
            pl.BlockSpec((devices, 1, modes_here, 2 * chan), lambda j: (0, j, 0, 0)),
            pl.BlockSpec((1, nlon, chan), lambda j: (j, 0, 0)),
        ],
        out_shape=[
            jax.ShapeDtypeStruct((devices, rows, modes_here, 2 * chan), BF),
            jax.ShapeDtypeStruct(field.shape, BF),
        ],
        compiler_params=pltpu.CompilerParams(vmem_limit_bytes=VMEM_LIMIT),
    )(field, gain.reshape(1, chan), table)


def middle_kernel(
    arrived_ref, fwd_ref, inv_ref, gain_ref, weight_ref, to_modes_ref, to_rows_ref, out_ref, by_mode, back
):
    devices, rows, modes_here, width = arrived_ref.shape
    flat = devices * modes_here
    for row in range(rows):
        block = arrived_ref[:, row].reshape(flat, width)
        by_mode[row] = dot(to_modes_ref[...], block).astype(BF)
    gain = jnp.concatenate([gain_ref[...], gain_ref[...]], axis=1)
    for mode in range(modes_here):
        here = slice(mode * devices, (mode + 1) * devices)
        spectrum = jnp.concatenate([by_mode[row, here] for row in range(rows)], axis=0)
        scaled = (dot(fwd_ref[mode], spectrum) * gain).astype(BF)
        synth = dot(inv_ref[mode], scaled).astype(BF)
        for row in range(rows):
            back[row, here] = synth[row * devices : (row + 1) * devices]
    for row in range(rows):
        block = dot(to_rows_ref[...], back[row]).astype(BF)
        mixed = dot(block, weight_ref[...]).astype(BF)
        out_ref[:, row] = mixed.reshape(devices, modes_here, width)


def middle(arrived, fwd, inv, gain, weight):
    devices, rows, modes_here, width = arrived.shape
    flat = devices * modes_here
    source = np.arange(flat).reshape(devices, modes_here).T.reshape(-1)
    to_modes = np.eye(flat, dtype=np.float32)[source].astype(ml_dtypes.bfloat16)
    return pl.pallas_call(
        middle_kernel,
        out_shape=jax.ShapeDtypeStruct(arrived.shape, BF),
        scratch_shapes=[
            pltpu.VMEM((rows, flat, width), BF),
            pltpu.VMEM((rows, flat, width), BF),
        ],
        compiler_params=pltpu.CompilerParams(vmem_limit_bytes=VMEM_LIMIT),
    )(arrived, fwd, inv, gain, weight, jnp.asarray(to_modes), jnp.asarray(np.ascontiguousarray(to_modes.T)))


def finish_kernel(
    synth_ref, normed_ref, field_ref, table_ref, gain_ref, up_ref, bias_ref, down_ref, out_ref, *, parts
):
    devices, unused, modes_here, width = synth_ref.shape
    chan = width // 2
    flat = synth_ref[:, 0].reshape(devices * modes_here, width)
    stacked = jnp.concatenate([flat[:, :chan], flat[:, chan:]], axis=0)
    size = field_ref.shape[1] // parts
    for part in range(parts):
        here = slice(part * size, (part + 1) * size)
        inner = dot(table_ref[here], stacked) + normed_ref[0, here].astype(F32)
        post = norm(inner, gain_ref[...]).astype(BF)
        hidden = jax.nn.gelu(dot(post, up_ref[...]) + bias_ref[...]).astype(BF)
        out = field_ref[0, here].astype(F32) + dot(hidden, down_ref[...])
        out_ref[0, here] = out.astype(BF)


def finish(synth, normed, field, table, gain, up, bias, down):
    devices, rows, modes_here, width = synth.shape
    nlon, chan = field.shape[1:]
    hidden = up.shape[1]
    whole = lambda a: pl.BlockSpec(a.shape, lambda j: (0,) * a.ndim)
    row_block = pl.BlockSpec((1, nlon, chan), lambda j: (j, 0, 0))
    gain = gain.reshape(1, chan)
    bias = bias.reshape(1, hidden)
    return pl.pallas_call(
        functools.partial(finish_kernel, parts=3),
        grid=(rows,),
        in_specs=[
            pl.BlockSpec((devices, 1, modes_here, width), lambda j: (0, j, 0, 0)),
            row_block,
            row_block,
            whole(table),
            whole(gain),
            whole(up),
            whole(bias),
            whole(down),
        ],
        out_specs=row_block,
        out_shape=jax.ShapeDtypeStruct(field.shape, BF),
        compiler_params=pltpu.CompilerParams(vmem_limit_bytes=VMEM_LIMIT),
    )(synth, normed, field, table, gain, up, bias, down)


def shards(
    field,
    norm_gain,
    legendre_fwd,
    legendre_inv,
    degree_gain,
    mix_weight,
    mlp_gain,
    up_weight,
    up_bias,
    down_weight,
    *,
    devices,
):
    rows, nlon, chan = field.shape
    modes_here, degrees, all_lats = legendre_fwd.shape
    forward, inverse = tables(nlon, modes_here * devices)
    forward, inverse = jnp.asarray(forward), jnp.asarray(inverse)
    spec, normed = analyse(field, norm_gain, forward, devices, modes_here)
    arrived = lax.all_to_all(spec, "lat", split_axis=0, concat_axis=0, tiled=True)
    fwd = legendre_fwd.reshape(modes_here, degrees, devices, rows)
    fwd = fwd.transpose(0, 1, 3, 2).reshape(modes_here, degrees, all_lats)
    inv = legendre_inv.reshape(modes_here, degrees, devices, rows)
    inv = inv.transpose(0, 3, 2, 1).reshape(modes_here, all_lats, degrees)
    real, imag = mix_weight[0], mix_weight[1]
    weight = jnp.concatenate(
        [jnp.concatenate([real, imag], 1), jnp.concatenate([-imag, real], 1)], 0
    )
    back = middle(arrived, fwd, inv, degree_gain, weight)
    synth = lax.all_to_all(back, "lat", split_axis=0, concat_axis=0, tiled=True)
    return finish(synth, normed, field, inverse, mlp_gain, up_weight, up_bias, down_weight)


def solution(mesh):
    return jax.shard_map(
        functools.partial(shards, devices=mesh.shape["lat"]),
        mesh=mesh,
        in_specs=(
            P(("ens", "lat"), None, None),
            P(),
            P("lat", None, None),
            P("lat", None, None),
            P(),
            P(),
            P(),
            P(),
            P(),
            P(),
        ),
        out_specs=P(("ens", "lat"), None, None),
        check_vma=False,
    )
```

```python
import functools
import math

import jax
import jax.numpy as jnp
import ml_dtypes
import numpy as np
from jax import lax
from jax.experimental import pallas as pl
from jax.experimental.pallas import tpu as pltpu
from jax.sharding import PartitionSpec as P

BF = jnp.bfloat16
F32 = jnp.float32
EPS = 1e-05
VMEM_LIMIT = 48 * 1024 * 1024


def tables(nlon, modes):
    lon = np.arange(nlon)
    wave = np.arange(modes)
    phase = (wave[:, None] * lon[None, :] % nlon) * (2.0 * math.pi / nlon)
    scale = 2.0 * math.pi / nlon
    weight = np.where(wave == 0, 1.0, 2.0)[:, None]
    forward = np.concatenate([scale * np.cos(phase), -scale * np.sin(phase)], 0)
    inverse = np.concatenate([weight * np.cos(phase), -weight * np.sin(phase)], 0).T
    as_bf = lambda a: a.astype(np.float32).astype(ml_dtypes.bfloat16)
    return as_bf(forward), as_bf(inverse)


def dot(a, b):
    return jnp.dot(a, b, preferred_element_type=F32)


def norm(values, gain):
    center = values - jnp.mean(values, axis=-1, keepdims=True)
    spread = jnp.mean(center * center, axis=-1, keepdims=True)
    return center * lax.rsqrt(spread + EPS) * gain


def cost(flops):
    return pl.CostEstimate(flops=4 * flops, bytes_accessed=0, transcendentals=0)


def analyse_kernel(me_ref, field_ref, gain_ref, table_ref, spec_ref, normed_ref):
    devices, unused, modes_here, width = spec_ref.shape
    modes = devices * modes_here
    chan = field_ref.shape[-1]
    normed = norm(field_ref[0].astype(F32), gain_ref[...]).astype(BF)
    normed_ref[0] = normed
    spec = dot(table_ref[...], normed).astype(BF)
    for device in range(devices):
        slot = jnp.bitwise_xor(me_ref[0], device)
        here = slice(device * modes_here, (device + 1) * modes_here)
        spec_ref[slot, 0, :, :chan] = spec[:modes][here]
        spec_ref[slot, 0, :, chan:] = spec[modes:][here]


def analyse(me, field, gain, table, devices, modes_here, first, rows):
    unused, nlon, chan = field.shape
    modes2 = table.shape[0]
    return pl.pallas_call(
        analyse_kernel,
        grid=(rows,),
        in_specs=[
            pl.BlockSpec(memory_space=pltpu.SMEM),
            pl.BlockSpec((1, nlon, chan), lambda j: (j + first, 0, 0)),
            pl.BlockSpec((1, chan), lambda j: (0, 0)),
            pl.BlockSpec((modes2, nlon), lambda j: (0, 0)),
        ],
        out_specs=[
            pl.BlockSpec((devices, 1, modes_here, 2 * chan), lambda j: (0, j, 0, 0)),
            pl.BlockSpec((1, nlon, chan), lambda j: (j, 0, 0)),
        ],
        out_shape=[
            jax.ShapeDtypeStruct((devices, rows, modes_here, 2 * chan), BF),
            jax.ShapeDtypeStruct((rows, nlon, chan), BF),
        ],
        compiler_params=pltpu.CompilerParams(vmem_limit_bytes=VMEM_LIMIT),
        cost_estimate=cost(2 * rows * modes2 * nlon * chan),
    )(me, field, gain.reshape(1, chan), table)


def prepare_kernel(fwd_ref, inv_ref, mix_ref, order_ref, fwd_out, inv_out, weight_out):
    chan = mix_ref.shape[-1]
    for mode in range(fwd_ref.shape[0]):
        fwd_out[mode] = dot(order_ref[...], fwd_ref[mode]).T.astype(BF)
        inv_out[mode] = dot(order_ref[...], inv_ref[mode]).astype(BF)
    weight_out[:chan, :chan] = mix_ref[0]
    weight_out[:chan, chan:] = mix_ref[1]
    weight_out[chan:, :chan] = -mix_ref[1]
    weight_out[chan:, chan:] = mix_ref[0]


def prepare(fwd, inv, mix, rows):
    modes_here, degrees, lats = fwd.shape
    chan = mix.shape[-1]
    order = np.arange(lats).reshape(lats // rows, rows).T.reshape(-1)
    order = np.eye(lats, dtype=np.float32)[order].astype(ml_dtypes.bfloat16)
    return pl.pallas_call(
        prepare_kernel,
        out_shape=[
            jax.ShapeDtypeStruct((modes_here, degrees, lats), BF),
            jax.ShapeDtypeStruct((modes_here, lats, degrees), BF),
            jax.ShapeDtypeStruct((2 * chan, 2 * chan), BF),
        ],
        compiler_params=pltpu.CompilerParams(vmem_limit_bytes=VMEM_LIMIT),
        cost_estimate=cost(4 * modes_here * degrees * lats * lats),
    )(fwd.transpose(0, 2, 1), inv.transpose(0, 2, 1), mix, jnp.asarray(order))


def middle_kernel(me_ref, *refs, chunks):
    arrived = refs[:chunks]
    fwd_ref, inv_ref, gain_ref, weight_ref, to_modes_ref, to_rows_ref = refs[chunks : chunks + 6]
    out = refs[chunks + 6 : 2 * chunks + 6]
    by_mode, back = refs[2 * chunks + 6 :]
    devices, unused, modes_here, width = arrived[0].shape
    places = [(ref, row) for ref in range(chunks) for row in range(arrived[ref].shape[1])]
    slots = [jnp.bitwise_xor(me_ref[0], device) for device in range(devices)]
    for at, (ref, row) in enumerate(places):
        block = jnp.concatenate([arrived[ref][slot, row] for slot in slots], axis=0)
        by_mode[at] = dot(to_modes_ref[...], block).astype(BF)
    gain = jnp.concatenate([gain_ref[...], gain_ref[...]], axis=1)
    for mode in range(modes_here):
        here = slice(mode * devices, (mode + 1) * devices)
        spectrum = jnp.concatenate([by_mode[at, here] for at in range(len(places))], axis=0)
        scaled = (dot(fwd_ref[mode], spectrum) * gain).astype(BF)
        synth = dot(inv_ref[mode], scaled).astype(BF)
        for at in range(len(places)):
            back[at, here] = synth[at * devices : (at + 1) * devices]
    for at, (ref, row) in enumerate(places):
        block = dot(to_rows_ref[...], back[at]).astype(BF)
        mixed = dot(block, weight_ref[...]).astype(BF)
        for device, slot in enumerate(slots):
            out[ref][slot, row] = mixed[device * modes_here : (device + 1) * modes_here]


def middle(me, arrived, fwd, inv, gain, weight):
    devices, unused, modes_here, width = arrived[0].shape
    rows = sum(a.shape[1] for a in arrived)
    flat = devices * modes_here
    source = np.arange(flat).reshape(devices, modes_here).T.reshape(-1)
    to_modes = np.eye(flat, dtype=np.float32)[source].astype(ml_dtypes.bfloat16)
    vmem = pl.BlockSpec(memory_space=pltpu.VMEM)
    return pl.pallas_call(
        functools.partial(middle_kernel, chunks=len(arrived)),
        in_specs=[pl.BlockSpec(memory_space=pltpu.SMEM)] + [vmem] * (len(arrived) + 6),
        out_specs=[vmem] * len(arrived),
        out_shape=[jax.ShapeDtypeStruct(a.shape, BF) for a in arrived],
        scratch_shapes=[
            pltpu.VMEM((rows, flat, width), BF),
            pltpu.VMEM((rows, flat, width), BF),
        ],
        compiler_params=pltpu.CompilerParams(vmem_limit_bytes=VMEM_LIMIT),
        cost_estimate=cost(4 * rows * flat * width * width),
    )(
        me,
        *arrived,
        fwd,
        inv,
        gain,
        weight,
        jnp.asarray(to_modes),
        jnp.asarray(np.ascontiguousarray(to_modes.T)),
    )


def finish_kernel(me_ref, synth_ref, normed_ref, field_ref, table_ref, gain_ref, up_ref, bias_ref, down_ref, *rest):
    out_ref, stacked = rest[-2:]
    devices, unused, modes_here, width = synth_ref.shape
    chan = width // 2
    modes = devices * modes_here
    for device in range(devices):
        slot = jnp.bitwise_xor(me_ref[0], device)
        at = device * modes_here
        stacked[at : at + modes_here] = synth_ref[slot, 0, :, :chan]
        stacked[modes + at : modes + at + modes_here] = synth_ref[slot, 0, :, chan:]
    inner = dot(table_ref[...], stacked[...]) + normed_ref[0].astype(F32)
    post = norm(inner, gain_ref[...]).astype(BF)
    hidden = jax.nn.gelu(dot(post, up_ref[...]) + bias_ref[...]).astype(BF)
    out_ref[0] = (field_ref[0].astype(F32) + dot(hidden, down_ref[...])).astype(BF)


def finish(me, synth, normed, field, table, gain, up, bias, down, first, result):
    devices, rows, modes_here, width = synth.shape
    nlon, chan = field.shape[1:]
    hidden = up.shape[1]
    whole = lambda a: pl.BlockSpec(a.shape, lambda j: (0,) * a.ndim)
    gain = gain.reshape(1, chan)
    bias = bias.reshape(1, hidden)
    placed = pl.BlockSpec((1, nlon, chan), lambda j: (j + first, 0, 0))
    operands = [me, synth, normed, field, table, gain, up, bias, down]
    specs = [
        pl.BlockSpec(memory_space=pltpu.SMEM),
        pl.BlockSpec((devices, 1, modes_here, width), lambda j: (0, j, 0, 0)),
        pl.BlockSpec((1, nlon, chan), lambda j: (j, 0, 0)),
        placed,
        whole(table),
        whole(gain),
        whole(up),
        whole(bias),
        whole(down),
    ]
    aliases = {}
    if result is not None:
        aliases = {len(operands): 0}
        operands.append(result)
        specs.append(pl.BlockSpec(memory_space=pl.ANY))
    return pl.pallas_call(
        finish_kernel,
        grid=(rows,),
        in_specs=specs,
        out_specs=placed,
        out_shape=jax.ShapeDtypeStruct(field.shape, BF),
        scratch_shapes=[pltpu.VMEM((2 * devices * modes_here, chan), BF)],
        input_output_aliases=aliases,
        compiler_params=pltpu.CompilerParams(vmem_limit_bytes=VMEM_LIMIT),
        cost_estimate=cost(2 * rows * nlon * chan * (devices * modes_here * 2 + 2 * hidden)),
    )(*operands)


NEAR = 2


def staged(devices):
    return devices % NEAR == 0 and devices & (devices - 1) == 0 and 8 <= devices <= 32


def swap(part, offset, devices):
    return lax.ppermute(part, "lat", [(a, a ^ offset) for a in range(devices)])


def after(values, early):
    return lax.optimization_barrier((values, early))[0]


def swap_near(blocks, devices):
    blocks = blocks.reshape((devices // NEAR, NEAR) + blocks.shape[1:])
    parts = [blocks[:, :1]]
    parts += [swap(blocks[:, k : k + 1], k, devices) for k in range(1, NEAR)]
    return jnp.concatenate(parts, 1)


def swap_far(blocks, devices):
    count = blocks.shape[0]
    parts = [blocks[:1]] + [None] * (count - 1)
    for k in range(count - 1, 0, -1):
        parts[k] = swap(blocks[k : k + 1], k * NEAR, devices)
    return parts


def joined(parts):
    blocks = jnp.concatenate(parts, 0)
    return blocks.reshape((-1,) + blocks.shape[2:])


def shards(
    field,
    norm_gain,
    legendre_fwd,
    legendre_inv,
    degree_gain,
    mix_weight,
    mlp_gain,
    up_weight,
    up_bias,
    down_weight,
    *,
    devices,
):
    rows, nlon, chan = field.shape
    modes_here, degrees, all_lats = legendre_fwd.shape
    forward, inverse = tables(nlon, modes_here * devices)
    forward, inverse = jnp.asarray(forward), jnp.asarray(inverse)
    me = jnp.zeros((1,), jnp.int32)
    if staged(devices):
        me = lax.axis_index("lat").astype(jnp.int32).reshape(1)
    take = lambda me, first, count: analyse(
        me, field, norm_gain, forward, devices, modes_here, first, count
    )
    give = lambda at, synth, result: finish(
        me, synth, normed[at], field, inverse, mlp_gain, up_weight, up_bias, down_weight, chunks[at][0], result
    )
    half = rows // 2
    chunks = [(0, half), (half, rows - half)]
    if not staged(devices):
        move = lambda blocks: lax.all_to_all(blocks, "lat", 0, 0, tiled=True)
        spec, normed = zip(*[take(me, *chunk) for chunk in chunks])
        fwd, inv, weight = prepare(legendre_fwd, legendre_inv, mix_weight, rows)
        back = middle(me, [move(blocks) for blocks in spec], fwd, inv, degree_gain, weight)
        return give(1, move(back[1]), give(0, move(back[0]), None))
    spec_a, normed_a = take(me, *chunks[0])
    spec_a = swap_near(spec_a, devices)
    spec_b, normed_b = take(after(me, spec_a[:, 1:]), *chunks[1])
    parts_a = swap_far(spec_a, devices)
    spec_b = swap_near(spec_b, devices)
    parts_b = swap_far(spec_b, devices)
    normed = [normed_a, normed_b]
    fwd, inv, weight = prepare(legendre_fwd, legendre_inv, mix_weight, rows)
    back = middle(me, [joined(parts_a), joined(parts_b)], fwd, inv, degree_gain, weight)
    parts_c = swap_far(swap_near(back[0], devices), devices)
    parts_d = swap_far(swap_near(back[1], devices), devices)
    result = give(0, after(joined(parts_c), parts_d[len(parts_d) - 3 :]), None)
    return give(1, joined(parts_d), result)


def solution(mesh):
    return jax.shard_map(
        functools.partial(shards, devices=mesh.shape["lat"]),
        mesh=mesh,
        in_specs=(
            P(("ens", "lat"), None, None),
            P(),
            P("lat", None, None),
            P("lat", None, None),
            P(),
            P(),
            P(),
            P(),
            P(),
            P(),
        ),
        out_specs=P(("ens", "lat"), None, None),
        check_vma=False,
    )
```

```python
import functools
import math

import jax
import jax.numpy as jnp
import ml_dtypes
import numpy as np
from jax import lax
from jax.experimental import pallas as pl
from jax.experimental.pallas import tpu as pltpu
from jax.sharding import PartitionSpec as P

BF = jnp.bfloat16
F32 = jnp.float32
EPS = 1e-05
GELU_LINEAR = math.sqrt(2.0 / math.pi)
GELU_CUBIC = 0.044715 * GELU_LINEAR
VMEM_LIMIT = 16 * 1024 * 1024


def tables(nlon, modes):
    lon = np.arange(nlon)
    wave = np.arange(modes)
    phase = (wave[:, None] * lon[None, :] % nlon) * (2.0 * math.pi / nlon)
    scale = 2.0 * math.pi / nlon
    weight = np.where(wave == 0, 1.0, 2.0)[:, None]
    forward = np.concatenate([scale * np.cos(phase), -scale * np.sin(phase)], 0)
    inverse = np.concatenate([weight * np.cos(phase), -weight * np.sin(phase)], 0).T
    as_bf = lambda a: a.astype(np.float32).astype(ml_dtypes.bfloat16)
    return as_bf(forward), as_bf(inverse)


def dot(a, b):
    return jnp.dot(a, b, preferred_element_type=F32)


def norm(values, gain):
    center = values - jnp.mean(values, axis=-1, keepdims=True)
    spread = jnp.mean(center * center, axis=-1, keepdims=True)
    return center * lax.rsqrt(spread + EPS) * gain


def cost(flops):
    return pl.CostEstimate(flops=4 * flops, bytes_accessed=0, transcendentals=0)


def analyse_kernel(me_ref, field_ref, gain_ref, table_ref, spec_ref, normed_ref):
    devices, unused, modes_here, width = spec_ref.shape
    modes = devices * modes_here
    chan = field_ref.shape[-1]
    normed = norm(field_ref[0].astype(F32), gain_ref[...]).astype(BF)
    normed_ref[0] = normed
    spec = dot(table_ref[...], normed).astype(BF)
    for device in range(devices):
        slot = jnp.bitwise_xor(me_ref[0], device)
        here = slice(device * modes_here, (device + 1) * modes_here)
        spec_ref[slot, 0, :, :chan] = spec[:modes][here]
        spec_ref[slot, 0, :, chan:] = spec[modes:][here]


def analyse(me, field, gain, table, devices, modes_here, first, rows):
    unused, nlon, chan = field.shape
    modes2 = table.shape[0]
    return pl.pallas_call(
        analyse_kernel,
        grid=(rows,),
        in_specs=[
            pl.BlockSpec(memory_space=pltpu.SMEM),
            pl.BlockSpec((1, nlon, chan), lambda j: (j + first, 0, 0)),
            pl.BlockSpec((1, chan), lambda j: (0, 0)),
            pl.BlockSpec((modes2, nlon), lambda j: (0, 0)),
        ],
        out_specs=[
            pl.BlockSpec((devices, 1, modes_here, 2 * chan), lambda j: (0, j, 0, 0)),
            pl.BlockSpec((1, nlon, chan), lambda j: (j, 0, 0)),
        ],
        out_shape=[
            jax.ShapeDtypeStruct((devices, rows, modes_here, 2 * chan), BF),
            jax.ShapeDtypeStruct((rows, nlon, chan), BF),
        ],
        compiler_params=pltpu.CompilerParams(vmem_limit_bytes=VMEM_LIMIT),
        cost_estimate=cost(2 * rows * modes2 * nlon * chan),
    )(me, pltpu.with_memory_space_constraint(field, pltpu.HBM), gain.reshape(1, chan), pltpu.with_memory_space_constraint(table, pltpu.HBM))


def prepare_kernel(fwd_ref, inv_ref, mix_ref, order_ref, fwd_out, inv_out, weight_out):
    chan = mix_ref.shape[-1]
    for mode in range(fwd_ref.shape[0]):
        fwd_out[mode] = dot(order_ref[...], fwd_ref[mode]).T.astype(BF)
        inv_out[mode] = dot(order_ref[...], inv_ref[mode]).astype(BF)
    weight_out[:chan, :chan] = mix_ref[0]
    weight_out[:chan, chan:] = mix_ref[1]
    weight_out[chan:, :chan] = -mix_ref[1]
    weight_out[chan:, chan:] = mix_ref[0]


def prepare(fwd, inv, mix, rows):
    modes_here, degrees, lats = fwd.shape
    chan = mix.shape[-1]
    order = np.arange(lats).reshape(lats // rows, rows).T.reshape(-1)
    order = np.eye(lats, dtype=np.float32)[order].astype(ml_dtypes.bfloat16)
    return pl.pallas_call(
        prepare_kernel,
        out_shape=[
            jax.ShapeDtypeStruct((modes_here, degrees, lats), BF),
            jax.ShapeDtypeStruct((modes_here, lats, degrees), BF),
            jax.ShapeDtypeStruct((2 * chan, 2 * chan), BF),
        ],
        compiler_params=pltpu.CompilerParams(vmem_limit_bytes=VMEM_LIMIT),
        cost_estimate=cost(4 * modes_here * degrees * lats * lats),
    )(fwd.transpose(0, 2, 1), inv.transpose(0, 2, 1), mix, jnp.asarray(order))


def middle_kernel(me_ref, *refs, chunks):
    arrived = refs[:chunks]
    fwd_ref, inv_ref, gain_ref, weight_ref, to_modes_ref, to_rows_ref = refs[chunks : chunks + 6]
    out = refs[chunks + 6 : 2 * chunks + 6]
    by_mode, back = refs[2 * chunks + 6 :]
    devices, unused, modes_here, width = arrived[0].shape
    places = [(ref, row) for ref in range(chunks) for row in range(arrived[ref].shape[1])]
    slots = [jnp.bitwise_xor(me_ref[0], device) for device in range(devices)]
    for at, (ref, row) in enumerate(places):
        block = jnp.concatenate([arrived[ref][slot, row] for slot in slots], axis=0)
        by_mode[at] = dot(to_modes_ref[...], block).astype(BF)
    gain = jnp.concatenate([gain_ref[...], gain_ref[...]], axis=1)
    for mode in range(modes_here):
        here = slice(mode * devices, (mode + 1) * devices)
        spectrum = jnp.concatenate([by_mode[at, here] for at in range(len(places))], axis=0)
        scaled = (dot(fwd_ref[mode], spectrum) * gain).astype(BF)
        synth = dot(inv_ref[mode], scaled).astype(BF)
        for at in range(len(places)):
            back[at, here] = synth[at * devices : (at + 1) * devices]
    for at, (ref, row) in enumerate(places):
        block = dot(to_rows_ref[...], back[at]).astype(BF)
        mixed = dot(block, weight_ref[...]).astype(BF)
        for device, slot in enumerate(slots):
            out[ref][slot, row] = mixed[device * modes_here : (device + 1) * modes_here]


def middle(me, arrived, fwd, inv, gain, weight):
    devices, unused, modes_here, width = arrived[0].shape
    rows = sum(a.shape[1] for a in arrived)
    flat = devices * modes_here
    source = np.arange(flat).reshape(devices, modes_here).T.reshape(-1)
    to_modes = np.eye(flat, dtype=np.float32)[source].astype(ml_dtypes.bfloat16)
    vmem = pl.BlockSpec(memory_space=pltpu.VMEM)
    return pl.pallas_call(
        functools.partial(middle_kernel, chunks=len(arrived)),
        in_specs=[pl.BlockSpec(memory_space=pltpu.SMEM)] + [vmem] * (len(arrived) + 6),
        out_specs=[vmem] * len(arrived),
        out_shape=[jax.ShapeDtypeStruct(a.shape, BF) for a in arrived],
        scratch_shapes=[
            pltpu.VMEM((rows, flat, width), BF),
            pltpu.VMEM((rows, flat, width), BF),
        ],
        compiler_params=pltpu.CompilerParams(vmem_limit_bytes=VMEM_LIMIT),
        cost_estimate=cost(4 * rows * flat * width * width),
    )(
        me,
        *arrived,
        fwd,
        inv,
        gain,
        weight,
        jnp.asarray(to_modes),
        jnp.asarray(np.ascontiguousarray(to_modes.T)),
    )


def gelu(x):
    inner = x * (GELU_LINEAR + GELU_CUBIC * (x * x))
    half = 0.5 * x
    return half + half * jnp.tanh(inner)


def finish_kernel(me_ref, synth_ref, normed_ref, field_ref, table_ref, gain_ref, up_ref, bias_ref, down_ref, *rest):
    out_ref, stacked = rest[-2:]
    devices, unused, modes_here, width = synth_ref.shape
    chan = width // 2
    modes = devices * modes_here
    for device in range(devices):
        slot = jnp.bitwise_xor(me_ref[0], device)
        at = device * modes_here
        stacked[at : at + modes_here] = synth_ref[slot, 0, :, :chan]
        stacked[modes + at : modes + at + modes_here] = synth_ref[slot, 0, :, chan:]
    inner = dot(table_ref[...], stacked[...]) + normed_ref[0].astype(F32)
    post = norm(inner, gain_ref[...]).astype(BF)
    size = post.shape[0] // 2
    for at in (0, size):
        here = slice(at, at + size)
        hidden = gelu((dot(post[here], up_ref[...]) + bias_ref[...]).astype(BF))
        out_ref[0, here] = (field_ref[0, here].astype(F32) + dot(hidden, down_ref[...])).astype(BF)


def finish(me, synth, normed, field, table, gain, up, bias, down, first, result):
    devices, rows, modes_here, width = synth.shape
    nlon, chan = field.shape[1:]
    hidden = up.shape[1]
    whole = lambda a: pl.BlockSpec(a.shape, lambda j: (0,) * a.ndim)
    gain = gain.reshape(1, chan)
    bias = bias.reshape(1, hidden)
    placed = pl.BlockSpec((1, nlon, chan), lambda j: (j + first, 0, 0))
    operands = [me, synth, normed, field, table, gain, up, bias, down]
    specs = [
        pl.BlockSpec(memory_space=pltpu.SMEM),
        pl.BlockSpec((devices, 1, modes_here, width), lambda j: (0, j, 0, 0)),
        pl.BlockSpec((1, nlon, chan), lambda j: (j, 0, 0)),
        placed,
        whole(table),
        whole(gain),
        whole(up),
        whole(bias),
        whole(down),
    ]
    aliases = {}
    if result is not None:
        aliases = {len(operands): 0}
        operands.append(result)
        specs.append(pl.BlockSpec(memory_space=pl.ANY))
    return pl.pallas_call(
        finish_kernel,
        grid=(rows,),
        in_specs=specs,
        out_specs=placed,
        out_shape=jax.ShapeDtypeStruct(field.shape, BF),
        scratch_shapes=[pltpu.VMEM((2 * devices * modes_here, chan), BF)],
        input_output_aliases=aliases,
        compiler_params=pltpu.CompilerParams(vmem_limit_bytes=VMEM_LIMIT),
        cost_estimate=cost(2 * rows * nlon * chan * (devices * modes_here * 2 + 2 * hidden)),
    )(*operands)


NEAR = 2


def staged(devices):
    return devices % NEAR == 0 and devices & (devices - 1) == 0 and 8 <= devices <= 32


def swap(part, offset, devices):
    return lax.ppermute(part, "lat", [(a, a ^ offset) for a in range(devices)])


def after(values, early):
    return lax.optimization_barrier((values, early))[0]


def swap_near(blocks, devices):
    blocks = blocks.reshape((devices // NEAR, NEAR) + blocks.shape[1:])
    parts = [blocks[:, :1]]
    parts += [swap(blocks[:, k : k + 1], k, devices) for k in range(1, NEAR)]
    return jnp.concatenate(parts, 1)


def swap_far(blocks, devices):
    count = blocks.shape[0]
    parts = [blocks[:1]] + [None] * (count - 1)
    for k in range(count - 1, 0, -1):
        parts[k] = swap(blocks[k : k + 1], k * NEAR, devices)
    return parts


def joined(parts):
    blocks = jnp.concatenate(parts, 0)
    return blocks.reshape((-1,) + blocks.shape[2:])


def shards(
    field,
    norm_gain,
    legendre_fwd,
    legendre_inv,
    degree_gain,
    mix_weight,
    mlp_gain,
    up_weight,
    up_bias,
    down_weight,
    *,
    devices,
):
    rows, nlon, chan = field.shape
    modes_here, degrees, all_lats = legendre_fwd.shape
    forward, inverse = tables(nlon, modes_here * devices)
    forward, inverse = jnp.asarray(forward), jnp.asarray(inverse)
    me = jnp.zeros((1,), jnp.int32)
    if staged(devices):
        me = lax.axis_index("lat").astype(jnp.int32).reshape(1)
    take = lambda me, first, count: analyse(
        me, field, norm_gain, forward, devices, modes_here, first, count
    )
    give = lambda at, synth, result: finish(
        me, synth, normed[at], field, inverse, mlp_gain, up_weight, up_bias, down_weight, chunks[at][0], result
    )
    half = rows // 2
    chunks = [(0, half), (half, rows - half)]
    if not staged(devices):
        move = lambda blocks: lax.all_to_all(blocks, "lat", 0, 0, tiled=True)
        spec, normed = zip(*[take(me, *chunk) for chunk in chunks])
        fwd, inv, weight = prepare(legendre_fwd, legendre_inv, mix_weight, rows)
        back = middle(me, [move(blocks) for blocks in spec], fwd, inv, degree_gain, weight)
        return give(1, move(back[1]), give(0, move(back[0]), None))
    spec_a, normed_a = take(me, *chunks[0])
    spec_a = swap_near(spec_a, devices)
    spec_b, normed_b = take(after(me, spec_a[:, 1:]), *chunks[1])
    parts_a = swap_far(spec_a, devices)
    spec_b = swap_near(spec_b, devices)
    parts_b = swap_far(spec_b, devices)
    normed = [normed_a, normed_b]
    fwd, inv, weight = prepare(legendre_fwd, legendre_inv, mix_weight, rows)
    back = middle(me, [joined(parts_a), joined(parts_b)], fwd, inv, degree_gain, weight)
    parts_c = swap_far(swap_near(back[0], devices), devices)
    parts_d = swap_far(swap_near(back[1], devices), devices)
    result = give(0, after(joined(parts_c), parts_d[len(parts_d) - 3 :]), None)
    return give(1, joined(parts_d), result)


def solution(mesh):
    return jax.shard_map(
        functools.partial(shards, devices=mesh.shape["lat"]),
        mesh=mesh,
        in_specs=(
            P(("ens", "lat"), None, None),
            P(),
            P("lat", None, None),
            P("lat", None, None),
            P(),
            P(),
            P(),
            P(),
            P(),
            P(),
        ),
        out_specs=P(("ens", "lat"), None, None),
        check_vma=False,
    )
```

```python
import functools
import math

import jax
import jax.numpy as jnp
import ml_dtypes
import numpy as np
from jax import lax
from jax.experimental import pallas as pl
from jax.experimental.pallas import tpu as pltpu
from jax.sharding import PartitionSpec as P

BF = jnp.bfloat16
F32 = jnp.float32
EPS = 1e-05
GELU_LINEAR = math.sqrt(2.0 / math.pi)
GELU_CUBIC = 0.044715 * GELU_LINEAR
VMEM_LIMIT = 16 * 1024 * 1024


def tables(nlon, modes):
    lon = np.arange(nlon)
    wave = np.arange(modes)
    phase = (wave[:, None] * lon[None, :] % nlon) * (2.0 * math.pi / nlon)
    scale = 2.0 * math.pi / nlon
    weight = np.where(wave == 0, 1.0, 2.0)[:, None]
    forward = np.concatenate([scale * np.cos(phase), -scale * np.sin(phase)], 0)
    inverse = np.concatenate([weight * np.cos(phase), -weight * np.sin(phase)], 0).T
    as_bf = lambda a: a.astype(np.float32).astype(ml_dtypes.bfloat16)
    return as_bf(forward), as_bf(inverse)


def dot(a, b):
    return jnp.dot(a, b, preferred_element_type=F32)


def norm(values, gain):
    center = values - jnp.mean(values, axis=-1, keepdims=True)
    spread = jnp.mean(center * center, axis=-1, keepdims=True)
    return center * lax.rsqrt(spread + EPS) * gain


def cost(flops):
    return pl.CostEstimate(flops=4 * flops, bytes_accessed=0, transcendentals=0)


def analyse_kernel(me_ref, field_ref, gain_ref, table_ref, spec_ref, normed_ref):
    devices, unused, modes_here, width = spec_ref.shape
    modes = devices * modes_here
    chan = field_ref.shape[-1]
    normed = norm(field_ref[0].astype(F32), gain_ref[...]).astype(BF)
    normed_ref[0] = normed
    spec = dot(table_ref[...], normed).astype(BF)
    for device in range(devices):
        slot = jnp.bitwise_xor(me_ref[0], device)
        here = slice(device * modes_here, (device + 1) * modes_here)
        spec_ref[slot, 0, :, :chan] = spec[:modes][here]
        spec_ref[slot, 0, :, chan:] = spec[modes:][here]


def analyse(me, field, gain, table, devices, modes_here, first, rows):
    unused, nlon, chan = field.shape
    modes2 = table.shape[0]
    return pl.pallas_call(
        analyse_kernel,
        grid=(rows,),
        in_specs=[
            pl.BlockSpec(memory_space=pltpu.SMEM),
            pl.BlockSpec((1, nlon, chan), lambda j: (j + first, 0, 0)),
            pl.BlockSpec((1, chan), lambda j: (0, 0)),
            pl.BlockSpec((modes2, nlon), lambda j: (0, 0)),
        ],
        out_specs=[
            pl.BlockSpec((devices, 1, modes_here, 2 * chan), lambda j: (0, j, 0, 0)),
            pl.BlockSpec((1, nlon, chan), lambda j: (j, 0, 0)),
        ],
        out_shape=[
            jax.ShapeDtypeStruct((devices, rows, modes_here, 2 * chan), BF),
            jax.ShapeDtypeStruct((rows, nlon, chan), BF),
        ],
        compiler_params=pltpu.CompilerParams(vmem_limit_bytes=VMEM_LIMIT),
        cost_estimate=cost(2 * rows * modes2 * nlon * chan),
    )(me, pltpu.with_memory_space_constraint(field, pltpu.HBM), gain.reshape(1, chan), pltpu.with_memory_space_constraint(table, pltpu.HBM))


def prepare_kernel(fwd_ref, inv_ref, mix_ref, order_ref, fwd_out, inv_out, weight_out):
    chan = mix_ref.shape[-1]
    for mode in range(fwd_ref.shape[0]):
        fwd_out[mode] = dot(order_ref[...], fwd_ref[mode]).T.astype(BF)
        inv_out[mode] = dot(order_ref[...], inv_ref[mode]).astype(BF)
    weight_out[:chan, :chan] = mix_ref[0]
    weight_out[:chan, chan:] = mix_ref[1]
    weight_out[chan:, :chan] = -mix_ref[1]
    weight_out[chan:, chan:] = mix_ref[0]


def prepare(fwd, inv, mix, rows):
    modes_here, degrees, lats = fwd.shape
    chan = mix.shape[-1]
    order = np.arange(lats).reshape(lats // rows, rows).T.reshape(-1)
    order = np.eye(lats, dtype=np.float32)[order].astype(ml_dtypes.bfloat16)
    return pl.pallas_call(
        prepare_kernel,
        out_shape=[
            jax.ShapeDtypeStruct((modes_here, degrees, lats), BF),
            jax.ShapeDtypeStruct((modes_here, lats, degrees), BF),
            jax.ShapeDtypeStruct((2 * chan, 2 * chan), BF),
        ],
        compiler_params=pltpu.CompilerParams(vmem_limit_bytes=VMEM_LIMIT),
        cost_estimate=cost(4 * modes_here * degrees * lats * lats),
    )(fwd.transpose(0, 2, 1), inv.transpose(0, 2, 1), mix, jnp.asarray(order))


def middle_kernel(me_ref, *refs, chunks):
    arrived = refs[:chunks]
    fwd_ref, inv_ref, gain_ref, weight_ref, to_modes_ref, to_rows_ref = refs[chunks : chunks + 6]
    out = refs[chunks + 6 : 2 * chunks + 6]
    by_mode, back = refs[2 * chunks + 6 :]
    devices, unused, modes_here, width = arrived[0].shape
    places = [(ref, row) for ref in range(chunks) for row in range(arrived[ref].shape[1])]
    slots = [jnp.bitwise_xor(me_ref[0], device) for device in range(devices)]
    for at, (ref, row) in enumerate(places):
        block = jnp.concatenate([arrived[ref][slot, row] for slot in slots], axis=0)
        by_mode[at] = dot(to_modes_ref[...], block).astype(BF)
    gain = jnp.concatenate([gain_ref[...], gain_ref[...]], axis=1)
    for mode in range(modes_here):
        here = slice(mode * devices, (mode + 1) * devices)
        spectrum = jnp.concatenate([by_mode[at, here] for at in range(len(places))], axis=0)
        scaled = (dot(fwd_ref[mode], spectrum) * gain).astype(BF)
        synth = dot(inv_ref[mode], scaled).astype(BF)
        for at in range(len(places)):
            back[at, here] = synth[at * devices : (at + 1) * devices]
    for at, (ref, row) in enumerate(places):
        block = dot(to_rows_ref[...], back[at]).astype(BF)
        mixed = dot(block, weight_ref[...]).astype(BF)
        for device, slot in enumerate(slots):
            out[ref][slot, row] = mixed[device * modes_here : (device + 1) * modes_here]


def middle(me, arrived, fwd, inv, gain, weight):
    devices, unused, modes_here, width = arrived[0].shape
    rows = sum(a.shape[1] for a in arrived)
    flat = devices * modes_here
    source = np.arange(flat).reshape(devices, modes_here).T.reshape(-1)
    to_modes = np.eye(flat, dtype=np.float32)[source].astype(ml_dtypes.bfloat16)
    vmem = pl.BlockSpec(memory_space=pltpu.VMEM)
    return pl.pallas_call(
        functools.partial(middle_kernel, chunks=len(arrived)),
        in_specs=[pl.BlockSpec(memory_space=pltpu.SMEM)] + [vmem] * (len(arrived) + 6),
        out_specs=[vmem] * len(arrived),
        out_shape=[jax.ShapeDtypeStruct(a.shape, BF) for a in arrived],
        scratch_shapes=[
            pltpu.VMEM((rows, flat, width), BF),
            pltpu.VMEM((rows, flat, width), BF),
        ],
        compiler_params=pltpu.CompilerParams(vmem_limit_bytes=VMEM_LIMIT),
        cost_estimate=cost(4 * rows * flat * width * width),
    )(
        me,
        *arrived,
        fwd,
        inv,
        gain,
        weight,
        jnp.asarray(to_modes),
        jnp.asarray(np.ascontiguousarray(to_modes.T)),
    )


def gelu(x):
    inner = x * (GELU_LINEAR + GELU_CUBIC * (x * x))
    half = 0.5 * x
    return half + half * jnp.tanh(inner)


def finish_kernel(me_ref, synth_ref, normed_ref, field_ref, table_ref, gain_ref, up_ref, bias_ref, down_ref, *rest):
    out_ref, stacked = rest[-2:]
    devices, unused, modes_here, width = synth_ref.shape
    chan = width // 2
    modes = devices * modes_here
    for device in range(devices):
        slot = jnp.bitwise_xor(me_ref[0], device)
        at = device * modes_here
        stacked[at : at + modes_here] = synth_ref[slot, 0, :, :chan]
        stacked[modes + at : modes + at + modes_here] = synth_ref[slot, 0, :, chan:]
    inner = dot(table_ref[...], stacked[...]) + normed_ref[0].astype(F32)
    post = norm(inner, gain_ref[...]).astype(BF)
    size = post.shape[0] // 2
    for at in (0, size):
        here = slice(at, at + size)
        hidden = gelu((dot(post[here], up_ref[...]) + bias_ref[...]).astype(BF))
        out_ref[0, here] = (field_ref[0, here].astype(F32) + dot(hidden, down_ref[...])).astype(BF)


def finish(me, synth, normed, field, table, gain, up, bias, down, first, result):
    devices, rows, modes_here, width = synth.shape
    nlon, chan = field.shape[1:]
    hidden = up.shape[1]
    whole = lambda a: pl.BlockSpec(a.shape, lambda j: (0,) * a.ndim)
    gain = gain.reshape(1, chan)
    bias = bias.reshape(1, hidden)
    placed = pl.BlockSpec((1, nlon, chan), lambda j: (j + first, 0, 0))
    operands = [me, synth, normed, field, table, gain, up, bias, down]
    specs = [
        pl.BlockSpec(memory_space=pltpu.SMEM),
        pl.BlockSpec((devices, 1, modes_here, width), lambda j: (0, j, 0, 0)),
        pl.BlockSpec((1, nlon, chan), lambda j: (j, 0, 0)),
        placed,
        whole(table),
        whole(gain),
        whole(up),
        whole(bias),
        whole(down),
    ]
    aliases = {}
    if result is not None:
        aliases = {len(operands): 0}
        operands.append(result)
        specs.append(pl.BlockSpec(memory_space=pl.ANY))
    return pl.pallas_call(
        finish_kernel,
        grid=(rows,),
        in_specs=specs,
        out_specs=placed,
        out_shape=jax.ShapeDtypeStruct(field.shape, BF),
        scratch_shapes=[pltpu.VMEM((2 * devices * modes_here, chan), BF)],
        input_output_aliases=aliases,
        compiler_params=pltpu.CompilerParams(vmem_limit_bytes=VMEM_LIMIT),
        cost_estimate=cost(2 * rows * nlon * chan * (devices * modes_here * 2 + 2 * hidden)),
    )(*operands)


NEAR = 2


def staged(devices):
    return devices % NEAR == 0 and devices & (devices - 1) == 0 and 8 <= devices <= 32


def swap(part, offset, devices):
    return lax.ppermute(part, "lat", [(a, a ^ offset) for a in range(devices)])


def after(values, early):
    return lax.optimization_barrier((values, early))[0]


def swap_near(blocks, devices):
    blocks = blocks.reshape((devices // NEAR, NEAR) + blocks.shape[1:])
    parts = [blocks[:, :1]]
    parts += [swap(blocks[:, k : k + 1], k, devices) for k in range(1, NEAR)]
    return jnp.concatenate(parts, 1)


def swap_far(blocks, devices):
    count = blocks.shape[0]
    parts = [blocks[:1]] + [None] * (count - 1)
    for k in (6, 1, 5, 2, 4, 3, 7):
        parts[k] = swap(blocks[k : k + 1], k * NEAR, devices)
    return parts


def joined(parts):
    blocks = jnp.concatenate(parts, 0)
    return blocks.reshape((-1,) + blocks.shape[2:])


def shards(
    field,
    norm_gain,
    legendre_fwd,
    legendre_inv,
    degree_gain,
    mix_weight,
    mlp_gain,
    up_weight,
    up_bias,
    down_weight,
    *,
    devices,
):
    rows, nlon, chan = field.shape
    modes_here, degrees, all_lats = legendre_fwd.shape
    forward, inverse = tables(nlon, modes_here * devices)
    forward, inverse = jnp.asarray(forward), jnp.asarray(inverse)
    me = jnp.zeros((1,), jnp.int32)
    if staged(devices):
        me = lax.axis_index("lat").astype(jnp.int32).reshape(1)
    take = lambda me, first, count: analyse(
        me, field, norm_gain, forward, devices, modes_here, first, count
    )
    give = lambda at, synth, result: finish(
        me, synth, normed[at], field, inverse, mlp_gain, up_weight, up_bias, down_weight, chunks[at][0], result
    )
    half = rows // 2
    chunks = [(0, half), (half, rows - half)]
    if not staged(devices):
        move = lambda blocks: lax.all_to_all(blocks, "lat", 0, 0, tiled=True)
        spec, normed = zip(*[take(me, *chunk) for chunk in chunks])
        fwd, inv, weight = prepare(legendre_fwd, legendre_inv, mix_weight, rows)
        back = middle(me, [move(blocks) for blocks in spec], fwd, inv, degree_gain, weight)
        return give(1, move(back[1]), give(0, move(back[0]), None))
    spec_a, normed_a = take(me, *chunks[0])
    spec_a = swap_near(spec_a, devices)
    spec_b, normed_b = take(after(me, spec_a[:, 1:]), *chunks[1])
    parts_a = swap_far(spec_a, devices)
    spec_b = swap_near(spec_b, devices)
    parts_b = swap_far(spec_b, devices)
    normed = [normed_a, normed_b]
    fwd, inv, weight = prepare(legendre_fwd, legendre_inv, mix_weight, rows)
    back = middle(me, [joined(parts_a), joined(parts_b)], fwd, inv, degree_gain, weight)
    parts_c = swap_far(swap_near(back[0], devices), devices)
    parts_d = swap_far(swap_near(back[1], devices), devices)
    result = give(0, after(joined(parts_c), [parts_d[k] for k in (1,7,)]), None)
    return give(1, joined(parts_d), result)


def solution(mesh):
    return jax.shard_map(
        functools.partial(shards, devices=mesh.shape["lat"]),
        mesh=mesh,
        in_specs=(
            P(("ens", "lat"), None, None),
            P(),
            P("lat", None, None),
            P("lat", None, None),
            P(),
            P(),
            P(),
            P(),
            P(),
            P(),
        ),
        out_specs=P(("ens", "lat"), None, None),
        check_vma=False,
    )
```

```python
import functools
import math

import jax
import jax.numpy as jnp
import ml_dtypes
import numpy as np
from jax import lax
from jax.experimental import pallas as pl
from jax.experimental.pallas import tpu as pltpu
from jax.sharding import PartitionSpec as P

BF = jnp.bfloat16
F32 = jnp.float32
EPS = 1e-05
GELU_LINEAR = math.sqrt(2.0 / math.pi)
GELU_CUBIC = 0.044715 * GELU_LINEAR
VMEM_LIMIT = 16 * 1024 * 1024


def tables(nlon, modes):
    lon = np.arange(nlon)
    wave = np.arange(modes)
    phase = (wave[:, None] * lon[None, :] % nlon) * (2.0 * math.pi / nlon)
    scale = 2.0 * math.pi / nlon
    weight = np.where(wave == 0, 1.0, 2.0)[:, None]
    forward = np.concatenate([scale * np.cos(phase), -scale * np.sin(phase)], 0)
    inverse = np.concatenate([weight * np.cos(phase), -weight * np.sin(phase)], 0).T
    as_bf = lambda a: a.astype(np.float32).astype(ml_dtypes.bfloat16)
    return as_bf(forward), as_bf(inverse)


def dot(a, b):
    return jnp.dot(a, b, preferred_element_type=F32)


def norm(values, gain):
    center = values - jnp.mean(values, axis=-1, keepdims=True)
    spread = jnp.mean(center * center, axis=-1, keepdims=True)
    return center * lax.rsqrt(spread + EPS) * gain


def cost(flops):
    return pl.CostEstimate(flops=4 * flops, bytes_accessed=0, transcendentals=0)


def analyse_kernel(me_ref, field_ref, gain_ref, table_ref, spec_ref, normed_ref):
    devices, unused, modes_here, width = spec_ref.shape
    modes = devices * modes_here
    chan = field_ref.shape[-1]
    normed = norm(field_ref[0].astype(F32), gain_ref[...]).astype(BF)
    normed_ref[0] = normed
    spec = dot(table_ref[...], normed).astype(BF)
    for device in range(devices):
        slot = jnp.bitwise_xor(me_ref[0], device)
        here = slice(device * modes_here, (device + 1) * modes_here)
        spec_ref[slot, 0, :, :chan] = spec[:modes][here]
        spec_ref[slot, 0, :, chan:] = spec[modes:][here]


def analyse(me, field, gain, table, devices, modes_here, first, rows):
    unused, nlon, chan = field.shape
    modes2 = table.shape[0]
    return pl.pallas_call(
        analyse_kernel,
        grid=(rows,),
        in_specs=[
            pl.BlockSpec(memory_space=pltpu.SMEM),
            pl.BlockSpec((1, nlon, chan), lambda j: (j + first, 0, 0)),
            pl.BlockSpec((chan,), lambda j: (0,)),
            pl.BlockSpec((modes2, nlon), lambda j: (0, 0)),
        ],
        out_specs=[
            pl.BlockSpec((devices, 1, modes_here, 2 * chan), lambda j: (0, j, 0, 0)),
            pl.BlockSpec((1, nlon, chan), lambda j: (j, 0, 0)),
        ],
        out_shape=[
            jax.ShapeDtypeStruct((devices, rows, modes_here, 2 * chan), BF),
            jax.ShapeDtypeStruct((rows, nlon, chan), BF),
        ],
        compiler_params=pltpu.CompilerParams(vmem_limit_bytes=VMEM_LIMIT),
        cost_estimate=cost(2 * rows * modes2 * nlon * chan),
    )(me, pltpu.with_memory_space_constraint(field, pltpu.HBM), pltpu.with_memory_space_constraint(gain, pltpu.HBM), pltpu.with_memory_space_constraint(table, pltpu.HBM))


def prepare_kernel(fwd_ref, inv_ref, mix_ref, order_ref, fwd_out, inv_out, weight_out):
    chan = mix_ref.shape[-1]
    for mode in range(fwd_ref.shape[0]):
        fwd_out[mode] = dot(order_ref[...], fwd_ref[mode]).T.astype(BF)
        inv_out[mode] = dot(order_ref[...], inv_ref[mode]).astype(BF)
    weight_out[:chan, :chan] = mix_ref[0]
    weight_out[:chan, chan:] = mix_ref[1]
    weight_out[chan:, :chan] = -mix_ref[1]
    weight_out[chan:, chan:] = mix_ref[0]


def prepare(fwd, inv, mix, rows):
    modes_here, degrees, lats = fwd.shape
    chan = mix.shape[-1]
    order = np.arange(lats).reshape(lats // rows, rows).T.reshape(-1)
    order = np.eye(lats, dtype=np.float32)[order].astype(ml_dtypes.bfloat16)
    return pl.pallas_call(
        prepare_kernel,
        out_shape=[
            jax.ShapeDtypeStruct((modes_here, degrees, lats), BF),
            jax.ShapeDtypeStruct((modes_here, lats, degrees), BF),
            jax.ShapeDtypeStruct((2 * chan, 2 * chan), BF),
        ],
        compiler_params=pltpu.CompilerParams(vmem_limit_bytes=VMEM_LIMIT),
        cost_estimate=cost(4 * modes_here * degrees * lats * lats),
    )(fwd.transpose(0, 2, 1), inv.transpose(0, 2, 1), mix, jnp.asarray(order))


def middle_kernel(me_ref, *refs, chunks):
    arrived = refs[:chunks]
    fwd_ref, inv_ref, gain_ref, weight_ref, to_modes_ref, to_rows_ref = refs[chunks : chunks + 6]
    out = refs[chunks + 6 : 2 * chunks + 6]
    by_mode, back = refs[2 * chunks + 6 :]
    devices, unused, modes_here, width = arrived[0].shape
    places = [(ref, row) for ref in range(chunks) for row in range(arrived[ref].shape[1])]
    slots = [jnp.bitwise_xor(me_ref[0], device) for device in range(devices)]
    for at, (ref, row) in enumerate(places):
        block = jnp.concatenate([arrived[ref][slot, row] for slot in slots], axis=0)
        by_mode[at] = dot(to_modes_ref[...], block).astype(BF)
    gain = jnp.concatenate([gain_ref[...], gain_ref[...]], axis=1)
    for mode in range(modes_here):
        here = slice(mode * devices, (mode + 1) * devices)
        spectrum = jnp.concatenate([by_mode[at, here] for at in range(len(places))], axis=0)
        scaled = (dot(fwd_ref[mode], spectrum) * gain).astype(BF)
        synth = dot(inv_ref[mode], scaled).astype(BF)
        for at in range(len(places)):
            back[at, here] = synth[at * devices : (at + 1) * devices]
    for at, (ref, row) in enumerate(places):
        block = dot(to_rows_ref[...], back[at]).astype(BF)
        mixed = dot(block, weight_ref[...]).astype(BF)
        for device, slot in enumerate(slots):
            out[ref][slot, row] = mixed[device * modes_here : (device + 1) * modes_here]


def middle(me, arrived, fwd, inv, gain, weight):
    devices, unused, modes_here, width = arrived[0].shape
    rows = sum(a.shape[1] for a in arrived)
    flat = devices * modes_here
    source = np.arange(flat).reshape(devices, modes_here).T.reshape(-1)
    to_modes = np.eye(flat, dtype=np.float32)[source].astype(ml_dtypes.bfloat16)
    vmem = pl.BlockSpec(memory_space=pltpu.VMEM)
    return pl.pallas_call(
        functools.partial(middle_kernel, chunks=len(arrived)),
        in_specs=[pl.BlockSpec(memory_space=pltpu.SMEM)] + [vmem] * (len(arrived) + 6),
        out_specs=[vmem] * len(arrived),
        out_shape=[jax.ShapeDtypeStruct(a.shape, BF) for a in arrived],
        scratch_shapes=[
            pltpu.VMEM((rows, flat, width), BF),
            pltpu.VMEM((rows, flat, width), BF),
        ],
        compiler_params=pltpu.CompilerParams(vmem_limit_bytes=VMEM_LIMIT),
        cost_estimate=cost(4 * rows * flat * width * width),
    )(
        me,
        *arrived,
        fwd,
        inv,
        gain,
        weight,
        jnp.asarray(to_modes),
        jnp.asarray(np.ascontiguousarray(to_modes.T)),
    )


def gelu(x):
    inner = x * (GELU_LINEAR + GELU_CUBIC * (x * x))
    half = 0.5 * x
    return half + half * jnp.tanh(inner)


def finish_kernel(me_ref, synth_ref, normed_ref, field_ref, table_ref, gain_ref, up_ref, bias_ref, down_ref, *rest):
    out_ref, stacked = rest[-2:]
    devices, unused, modes_here, width = synth_ref.shape
    chan = width // 2
    modes = devices * modes_here
    for device in range(devices):
        slot = jnp.bitwise_xor(me_ref[0], device)
        at = device * modes_here
        stacked[at : at + modes_here] = synth_ref[slot, 0, :, :chan]
        stacked[modes + at : modes + at + modes_here] = synth_ref[slot, 0, :, chan:]
    inner = dot(table_ref[...], stacked[...]) + normed_ref[0].astype(F32)
    post = norm(inner, gain_ref[...]).astype(BF)
    size = post.shape[0] // 2
    for at in (0, size):
        here = slice(at, at + size)
        hidden = gelu((dot(post[here], up_ref[...]) + bias_ref[...]).astype(BF))
        out_ref[0, here] = (field_ref[0, here].astype(F32) + dot(hidden, down_ref[...])).astype(BF)


def finish(me, synth, normed, field, table, gain, up, bias, down, first, result):
    devices, rows, modes_here, width = synth.shape
    nlon, chan = field.shape[1:]
    hidden = up.shape[1]
    whole = lambda a: pl.BlockSpec(a.shape, lambda j: (0,) * a.ndim)
    gain = gain.reshape(1, chan)
    bias = bias.reshape(1, hidden)
    placed = pl.BlockSpec((1, nlon, chan), lambda j: (j + first, 0, 0))
    operands = [me, synth, normed, field, table, gain, up, bias, down]
    specs = [
        pl.BlockSpec(memory_space=pltpu.SMEM),
        pl.BlockSpec((devices, 1, modes_here, width), lambda j: (0, j, 0, 0)),
        pl.BlockSpec((1, nlon, chan), lambda j: (j, 0, 0)),
        placed,
        whole(table),
        whole(gain),
        whole(up),
        whole(bias),
        whole(down),
    ]
    aliases = {}
    if result is not None:
        aliases = {len(operands): 0}
        operands.append(result)
        specs.append(pl.BlockSpec(memory_space=pl.ANY))
    return pl.pallas_call(
        finish_kernel,
        grid=(rows,),
        in_specs=specs,
        out_specs=placed,
        out_shape=jax.ShapeDtypeStruct(field.shape, BF),
        scratch_shapes=[pltpu.VMEM((2 * devices * modes_here, chan), BF)],
        input_output_aliases=aliases,
        compiler_params=pltpu.CompilerParams(vmem_limit_bytes=VMEM_LIMIT),
        cost_estimate=cost(2 * rows * nlon * chan * (devices * modes_here * 2 + 2 * hidden)),
    )(*operands)


NEAR = 2


def staged(devices):
    return devices % NEAR == 0 and devices & (devices - 1) == 0 and 8 <= devices <= 32


def swap(part, offset, devices):
    return lax.ppermute(part, "lat", [(a, a ^ offset) for a in range(devices)])


def after(values, early):
    return lax.optimization_barrier((values, early))[0]


def swap_near(blocks, devices):
    blocks = blocks.reshape((devices // NEAR, NEAR) + blocks.shape[1:])
    parts = [blocks[:, :1]]
    parts += [swap(blocks[:, k : k + 1], k, devices) for k in range(1, NEAR)]
    return jnp.concatenate(parts, 1)


def swap_far(blocks, devices):
    count = blocks.shape[0]
    parts = [blocks[:1]] + [None] * (count - 1)
    for k in (6, 1, 5, 2, 4, 3, 7):
        parts[k] = swap(blocks[k : k + 1], k * NEAR, devices)
    return parts


def joined(parts):
    blocks = jnp.concatenate(parts, 0)
    return blocks.reshape((-1,) + blocks.shape[2:])


def shards(
    field,
    norm_gain,
    legendre_fwd,
    legendre_inv,
    degree_gain,
    mix_weight,
    mlp_gain,
    up_weight,
    up_bias,
    down_weight,
    *,
    devices,
):
    rows, nlon, chan = field.shape
    modes_here, degrees, all_lats = legendre_fwd.shape
    forward, inverse = tables(nlon, modes_here * devices)
    forward, inverse = jnp.asarray(forward), jnp.asarray(inverse)
    me = jnp.zeros((1,), jnp.int32)
    if staged(devices):
        me = lax.axis_index("lat").astype(jnp.int32).reshape(1)
    take = lambda me, first, count: analyse(
        me, field, norm_gain, forward, devices, modes_here, first, count
    )
    give = lambda at, synth, result: finish(
        me, synth, normed[at], field, inverse, mlp_gain, up_weight, up_bias, down_weight, chunks[at][0], result
    )
    half = rows // 2
    chunks = [(0, half), (half, rows - half)]
    if not staged(devices):
        move = lambda blocks: lax.all_to_all(blocks, "lat", 0, 0, tiled=True)
        spec, normed = zip(*[take(me, *chunk) for chunk in chunks])
        fwd, inv, weight = prepare(legendre_fwd, legendre_inv, mix_weight, rows)
        back = middle(me, [move(blocks) for blocks in spec], fwd, inv, degree_gain, weight)
        return give(1, move(back[1]), give(0, move(back[0]), None))
    spec_a, normed_a = take(me, *chunks[0])
    spec_a = swap_near(spec_a, devices)
    spec_b, normed_b = take(after(me, spec_a[:, 1:]), *chunks[1])
    parts_a = swap_far(spec_a, devices)
    spec_b = swap_near(spec_b, devices)
    parts_b = swap_far(spec_b, devices)
    normed = [normed_a, normed_b]
    fwd, inv, weight = prepare(legendre_fwd, legendre_inv, mix_weight, rows)
    back = middle(me, [joined(parts_a), joined(parts_b)], fwd, inv, degree_gain, weight)
    parts_c = swap_far(swap_near(back[0], devices), devices)
    parts_d = swap_far(swap_near(back[1], devices), devices)
    result = give(0, after(joined(parts_c), [parts_d[k] for k in (1,7,)]), None)
    return give(1, joined(parts_d), result)


def solution(mesh):
    return jax.shard_map(
        functools.partial(shards, devices=mesh.shape["lat"]),
        mesh=mesh,
        in_specs=(
            P(("ens", "lat"), None, None),
            P(),
            P("lat", None, None),
            P("lat", None, None),
            P(),
            P(),
            P(),
            P(),
            P(),
            P(),
        ),
        out_specs=P(("ens", "lat"), None, None),
        check_vma=False,
    )
```

```python
import functools
import math

import jax
import jax.numpy as jnp
import ml_dtypes
import numpy as np
from jax import lax
from jax.experimental import pallas as pl
from jax.experimental.pallas import tpu as pltpu
from jax.sharding import PartitionSpec as P

BF = jnp.bfloat16
F32 = jnp.float32
EPS = 1e-05
GELU_LINEAR = math.sqrt(2.0 / math.pi)
GELU_CUBIC = 0.044715 * GELU_LINEAR
VMEM_LIMIT = 16 * 1024 * 1024


def tables(nlon, modes):
    lon = np.arange(nlon)
    wave = np.arange(modes)
    phase = (wave[:, None] * lon[None, :] % nlon) * (2.0 * math.pi / nlon)
    scale = 2.0 * math.pi / nlon
    weight = np.where(wave == 0, 1.0, 2.0)[:, None]
    forward = np.concatenate([scale * np.cos(phase), -scale * np.sin(phase)], 0)
    inverse = np.concatenate([weight * np.cos(phase), -weight * np.sin(phase)], 0).T
    as_bf = lambda a: a.astype(np.float32).astype(ml_dtypes.bfloat16)
    return as_bf(forward), as_bf(inverse)


def dot(a, b):
    return jnp.dot(a, b, preferred_element_type=F32)


def norm(values, gain):
    center = values - jnp.mean(values, axis=-1, keepdims=True)
    spread = jnp.mean(center * center, axis=-1, keepdims=True)
    return center * lax.rsqrt(spread + EPS) * gain


def cost(flops):
    return pl.CostEstimate(flops=4 * flops, bytes_accessed=0, transcendentals=0)


def analyse_kernel(me_ref, field_ref, gain_ref, table_ref, spec_ref, normed_ref):
    devices, unused, modes_here, width = spec_ref.shape
    modes = devices * modes_here
    chan = field_ref.shape[-1]
    normed = norm(field_ref[0].astype(F32), gain_ref[...]).astype(BF)
    normed_ref[0] = normed
    spec = dot(table_ref[...], normed).astype(BF)
    for device in range(devices):
        slot = jnp.bitwise_xor(me_ref[0], device)
        here = slice(device * modes_here, (device + 1) * modes_here)
        spec_ref[slot, 0, :, :chan] = spec[:modes][here]
        spec_ref[slot, 0, :, chan:] = spec[modes:][here]


def analyse(me, field, gain, table, devices, modes_here, first, rows):
    unused, nlon, chan = field.shape
    modes2 = table.shape[0]
    return pl.pallas_call(
        analyse_kernel,
        grid=(rows,),
        in_specs=[
            pl.BlockSpec(memory_space=pltpu.SMEM),
            pl.BlockSpec((1, nlon, chan), lambda j: (j + first, 0, 0)),
            pl.BlockSpec((chan,), lambda j: (0,)),
            pl.BlockSpec((modes2, nlon), lambda j: (0, 0)),
        ],
        out_specs=[
            pl.BlockSpec((devices, 1, modes_here, 2 * chan), lambda j: (0, j, 0, 0)),
            pl.BlockSpec((1, nlon, chan), lambda j: (j, 0, 0)),
        ],
        out_shape=[
            jax.ShapeDtypeStruct((devices, rows, modes_here, 2 * chan), BF),
            jax.ShapeDtypeStruct((rows, nlon, chan), BF),
        ],
        compiler_params=pltpu.CompilerParams(vmem_limit_bytes=VMEM_LIMIT),
        cost_estimate=cost(2 * rows * modes2 * nlon * chan),
    )(me, pltpu.with_memory_space_constraint(field, pltpu.HBM), pltpu.with_memory_space_constraint(gain, pltpu.HBM), pltpu.with_memory_space_constraint(table, pltpu.HBM))


def prepare_kernel(fwd_ref, inv_ref, mix_ref, order_ref, fwd_out, inv_out, weight_out):
    chan = mix_ref.shape[-1]
    for mode in range(fwd_ref.shape[0]):
        fwd_out[mode] = dot(order_ref[...], fwd_ref[mode]).T.astype(BF)
        inv_out[mode] = dot(order_ref[...], inv_ref[mode]).astype(BF)
    weight_out[:chan, :chan] = mix_ref[0]
    weight_out[:chan, chan:] = mix_ref[1]
    weight_out[chan:, :chan] = -mix_ref[1]
    weight_out[chan:, chan:] = mix_ref[0]


def prepare(fwd, inv, mix, rows):
    modes_here, degrees, lats = fwd.shape
    chan = mix.shape[-1]
    order = np.arange(lats).reshape(lats // rows, rows).T.reshape(-1)
    order = np.eye(lats, dtype=np.float32)[order].astype(ml_dtypes.bfloat16)
    return pl.pallas_call(
        prepare_kernel,
        out_shape=[
            jax.ShapeDtypeStruct((modes_here, degrees, lats), BF),
            jax.ShapeDtypeStruct((modes_here, lats, degrees), BF),
            jax.ShapeDtypeStruct((2 * chan, 2 * chan), BF),
        ],
        compiler_params=pltpu.CompilerParams(vmem_limit_bytes=VMEM_LIMIT),
        cost_estimate=cost(4 * modes_here * degrees * lats * lats),
    )(fwd.transpose(0, 2, 1), inv.transpose(0, 2, 1), mix, jnp.asarray(order))


def middle_kernel(me_ref, *refs, chunks):
    arrived = refs[:chunks]
    fwd_ref, inv_ref, gain_ref, weight_ref, to_modes_ref, to_rows_ref = refs[chunks : chunks + 6]
    out = refs[chunks + 6 : 2 * chunks + 6]
    by_mode, back = refs[2 * chunks + 6 :]
    devices, unused, modes_here, width = arrived[0].shape
    places = [(ref, row) for ref in range(chunks) for row in range(arrived[ref].shape[1])]
    slots = [jnp.bitwise_xor(me_ref[0], device) for device in range(devices)]
    for at, (ref, row) in enumerate(places):
        block = jnp.concatenate([arrived[ref][slot, row] for slot in slots], axis=0)
        by_mode[at] = dot(to_modes_ref[...], block).astype(BF)
    gain = jnp.concatenate([gain_ref[...], gain_ref[...]], axis=1)
    for mode in range(modes_here):
        here = slice(mode * devices, (mode + 1) * devices)
        spectrum = jnp.concatenate([by_mode[at, here] for at in range(len(places))], axis=0)
        scaled = (dot(fwd_ref[mode], spectrum) * gain).astype(BF)
        synth = dot(inv_ref[mode], scaled).astype(BF)
        for at in range(len(places)):
            back[at, here] = synth[at * devices : (at + 1) * devices]
    for at, (ref, row) in enumerate(places):
        block = dot(to_rows_ref[...], back[at]).astype(BF)
        mixed = dot(block, weight_ref[...]).astype(BF)
        for device, slot in enumerate(slots):
            out[ref][slot, row] = mixed[device * modes_here : (device + 1) * modes_here]


def middle(me, arrived, fwd, inv, gain, weight):
    devices, unused, modes_here, width = arrived[0].shape
    rows = sum(a.shape[1] for a in arrived)
    flat = devices * modes_here
    source = np.arange(flat).reshape(devices, modes_here).T.reshape(-1)
    to_modes = np.eye(flat, dtype=np.float32)[source].astype(ml_dtypes.bfloat16)
    vmem = pl.BlockSpec(memory_space=pltpu.VMEM)
    return pl.pallas_call(
        functools.partial(middle_kernel, chunks=len(arrived)),
        in_specs=[pl.BlockSpec(memory_space=pltpu.SMEM)] + [vmem] * (len(arrived) + 6),
        out_specs=[vmem] * len(arrived),
        out_shape=[jax.ShapeDtypeStruct(a.shape, BF) for a in arrived],
        scratch_shapes=[
            pltpu.VMEM((rows, flat, width), BF),
            pltpu.VMEM((rows, flat, width), BF),
        ],
        compiler_params=pltpu.CompilerParams(vmem_limit_bytes=VMEM_LIMIT),
        cost_estimate=cost(4 * rows * flat * width * width),
    )(
        me,
        *arrived,
        fwd,
        inv,
        gain,
        weight,
        jnp.asarray(to_modes),
        jnp.asarray(np.ascontiguousarray(to_modes.T)),
    )


def gelu(x):
    inner = x * (GELU_LINEAR + GELU_CUBIC * (x * x))
    half = 0.5 * x
    return half + half * jnp.tanh(inner)


def finish_kernel(me_ref, synth_ref, normed_ref, field_ref, table_ref, gain_ref, up_ref, bias_ref, down_ref, *rest):
    out_ref, stacked = rest[-2:]
    devices, unused, modes_here, width = synth_ref.shape
    chan = width // 2
    modes = devices * modes_here
    for device in range(devices):
        slot = jnp.bitwise_xor(me_ref[0], device)
        at = device * modes_here
        stacked[at : at + modes_here] = synth_ref[slot, 0, :, :chan]
        stacked[modes + at : modes + at + modes_here] = synth_ref[slot, 0, :, chan:]
    inner = dot(table_ref[...], stacked[...]) + normed_ref[0].astype(F32)
    post = norm(inner, gain_ref[...]).astype(BF)
    size = post.shape[0] // 3
    for at in (0, size, 2 * size):
        here = slice(at, at + size)
        hidden = gelu((dot(post[here], up_ref[...]) + bias_ref[...]).astype(BF))
        out_ref[0, here] = (field_ref[0, here].astype(F32) + dot(hidden, down_ref[...])).astype(BF)


def finish(me, synth, normed, field, table, gain, up, bias, down, first, result):
    devices, rows, modes_here, width = synth.shape
    nlon, chan = field.shape[1:]
    hidden = up.shape[1]
    whole = lambda a: pl.BlockSpec(a.shape, lambda j: (0,) * a.ndim)
    gain = gain.reshape(1, chan)
    bias = bias.reshape(1, hidden)
    placed = pl.BlockSpec((1, nlon, chan), lambda j: (j + first, 0, 0))
    operands = [me, synth, normed, field, table, gain, up, bias, down]
    specs = [
        pl.BlockSpec(memory_space=pltpu.SMEM),
        pl.BlockSpec((devices, 1, modes_here, width), lambda j: (0, j, 0, 0)),
        pl.BlockSpec((1, nlon, chan), lambda j: (j, 0, 0)),
        placed,
        whole(table),
        whole(gain),
        whole(up),
        whole(bias),
        whole(down),
    ]
    aliases = {}
    if result is not None:
        aliases = {len(operands): 0}
        operands.append(result)
        specs.append(pl.BlockSpec(memory_space=pl.ANY))
    return pl.pallas_call(
        finish_kernel,
        grid=(rows,),
        in_specs=specs,
        out_specs=placed,
        out_shape=jax.ShapeDtypeStruct(field.shape, BF),
        scratch_shapes=[pltpu.VMEM((2 * devices * modes_here, chan), BF)],
        input_output_aliases=aliases,
        compiler_params=pltpu.CompilerParams(vmem_limit_bytes=VMEM_LIMIT),
        cost_estimate=cost(2 * rows * nlon * chan * (devices * modes_here * 2 + 2 * hidden)),
    )(*operands)


NEAR = 2


def staged(devices):
    return devices % NEAR == 0 and devices & (devices - 1) == 0 and 8 <= devices <= 32


def swap(part, offset, devices):
    return lax.ppermute(part, "lat", [(a, a ^ offset) for a in range(devices)])


def after(values, early):
    return lax.optimization_barrier((values, early))[0]


def swap_near(blocks, devices):
    blocks = blocks.reshape((devices // NEAR, NEAR) + blocks.shape[1:])
    parts = [blocks[:, :1]]
    parts += [swap(blocks[:, k : k + 1], k, devices) for k in range(1, NEAR)]
    return jnp.concatenate(parts, 1)


def swap_far(blocks, devices):
    count = blocks.shape[0]
    parts = [blocks[:1]] + [None] * (count - 1)
    for k in (6, 1, 5, 2, 4, 3, 7):
        parts[k] = swap(blocks[k : k + 1], k * NEAR, devices)
    return parts


def joined(parts):
    blocks = jnp.concatenate(parts, 0)
    return blocks.reshape((-1,) + blocks.shape[2:])


def shards(
    field,
    norm_gain,
    legendre_fwd,
    legendre_inv,
    degree_gain,
    mix_weight,
    mlp_gain,
    up_weight,
    up_bias,
    down_weight,
    *,
    devices,
):
    rows, nlon, chan = field.shape
    modes_here, degrees, all_lats = legendre_fwd.shape
    forward, inverse = tables(nlon, modes_here * devices)
    forward, inverse = jnp.asarray(forward), jnp.asarray(inverse)
    me = jnp.zeros((1,), jnp.int32)
    if staged(devices):
        me = lax.axis_index("lat").astype(jnp.int32).reshape(1)
    take = lambda me, first, count: analyse(
        me, field, norm_gain, forward, devices, modes_here, first, count
    )
    give = lambda at, synth, result: finish(
        me, synth, normed[at], field, inverse, mlp_gain, up_weight, up_bias, down_weight, chunks[at][0], result
    )
    half = rows // 2
    chunks = [(0, half), (half, rows - half)]
    if not staged(devices):
        move = lambda blocks: lax.all_to_all(blocks, "lat", 0, 0, tiled=True)
        spec, normed = zip(*[take(me, *chunk) for chunk in chunks])
        fwd, inv, weight = prepare(legendre_fwd, legendre_inv, mix_weight, rows)
        back = middle(me, [move(blocks) for blocks in spec], fwd, inv, degree_gain, weight)
        return give(1, move(back[1]), give(0, move(back[0]), None))
    spec_a, normed_a = take(me, *chunks[0])
    spec_a = swap_near(spec_a, devices)
    spec_b, normed_b = take(after(me, spec_a[:, 1:]), *chunks[1])
    parts_a = swap_far(spec_a, devices)
    spec_b = swap_near(spec_b, devices)
    parts_b = swap_far(spec_b, devices)
    normed = [normed_a, normed_b]
    fwd, inv, weight = prepare(legendre_fwd, legendre_inv, mix_weight, rows)
    back = middle(me, [joined(parts_a), joined(parts_b)], fwd, inv, degree_gain, weight)
    parts_c = swap_far(swap_near(back[0], devices), devices)
    parts_d = swap_far(swap_near(back[1], devices), devices)
    result = give(0, after(joined(parts_c), [parts_d[k] for k in (1,7,)]), None)
    return give(1, joined(parts_d), result)


def solution(mesh):
    return jax.shard_map(
        functools.partial(shards, devices=mesh.shape["lat"]),
        mesh=mesh,
        in_specs=(
            P(("ens", "lat"), None, None),
            P(),
            P("lat", None, None),
            P("lat", None, None),
            P(),
            P(),
            P(),
            P(),
            P(),
            P(),
        ),
        out_specs=P(("ens", "lat"), None, None),
        check_vma=False,
    )
```
